32 devices in a mesh: seq: 16 (over z, y, x), tp: 2 (over core).
Axes of the slice: x: 2, y: 2, z: 4, core: 2. Of those that a mesh axis runs over, the one named last changes fastest.
Arguments:
- x_resid: bfloat16 [2048, 2880], P('seq', 'tp'), may hold values from -6 to 6
- q_new: bfloat16 [2048, 4096], P('seq', 'tp'), may hold values from -10 to 12
- kv_new: bfloat16 [2048, 8, 128], P('seq', 'tp'), may hold values from -4 to 4
- kv_cache: bfloat16 [512, 32, 8, 128], P('seq', None, 'tp'), may hold values from -4 to 11.5
- cache_len: int32 [16], replicated, may hold values from 0 to 1024, as said below
- page_table: int32 [16, 32], replicated, may hold values from 0 to 511, as said below
- sinks: float32 [64], P('tp'), may hold values from 0 to 8
- out_weight: bfloat16 [4096, 2880], P('tp'), may hold values from -0.09375 to 0.09375
- norm_gain: float32 [2880], replicated, may hold values from 0.1 to 1.9
- routes: int32 [2048, 4], P('seq'), may hold values from 0 to 15, all different within a row; in each aligned block of 128 rows (0 to 127, 128 to 255, ...) at most 64 rows name the same one
- route_wt: float32 [2048, 4], P('seq'), may hold values from 0.05 to 0.5
- w_gate: bfloat16 [16, 2880, 2880], P('seq', None, 'tp'), may hold values from -0.109375 to 0.109375
- w_up: bfloat16 [16, 2880, 2880], P('seq', None, 'tp'), may hold values from -0.109375 to 0.109375
- w_down: bfloat16 [16, 2880, 2880], P('seq', 'tp'), may hold values from -0.109375 to 0.109375
Outputs:
- attended: bfloat16 [2048, 4096], P('seq', 'tp')
- output: bfloat16 [2048, 2880], P('seq', 'tp')
The draws below stay inside these ranges and needn't reach their ends.
Inputs may be any that keep to these rules, and one draw needn't show every extreme that they name: `routes`: each row names 4 different experts; in each aligned block of 128 rows no expert is named by more than 64 rows. `cache_len`: the largest is exactly 1024. `page_table`: every pool page appears exactly once; pool pages d * 32 to (d + 1) * 32 - 1 hold exactly 2 pages of each request.
All inputs are finite; a program needn't handle non-finite values.
Results may differ from the reference program's by a relative error of at most 0.02.
Values may be sent and summed in bfloat16 or wider, within the bound.
A program may use at most 128 MiB of HBM per device.

```python
import math
import jax
import jax.numpy as jnp
import numpy as np
from jax import lax

D = 2880
QH = 64
KVH = 8
HEAD = 64
EF = 2880
TOPK = 4
NEW = 128
MAXC = 1024
PAGE = 32
TOK_DEV = 128
EXPERTS = 16
TOKENS = 2048
REQUESTS = 16
MAXP = 32
SLOTS = 32
KPG = 2
CAP = 64
QPK = 8
N_SEQ = 16
N_TP = 2


def draw_q_new(key, part):
    first = jax.random.fold_in(key, 0)
    base = 2.5 * jnp.clip(jax.random.normal(first, (TOKENS, QH, HEAD), jnp.float32), -4.0, 4.0)
    return base.reshape(TOKENS, QH * HEAD).astype(jnp.bfloat16)


def draw_kv_cache(key, part):
    first = jax.random.fold_in(key, 0)
    pool = SLOTS * (MAXP // KPG)
    shape = (pool, PAGE, KVH, 2 * HEAD)
    base = jnp.clip(jax.random.normal(first, shape, jnp.float32), -4.0, 4.0)
    return base.astype(jnp.bfloat16)


def draw_cache_len(key, part):
    first, second, third = jax.random.split(key, 3)
    left = jax.random.randint(first, (REQUESTS,), 0, MAXC + 1)
    right = jax.random.randint(second, (REQUESTS,), 0, MAXC + 1)
    lengths = left * right // MAXC
    longest = jax.random.randint(third, (), 0, REQUESTS)
    return jnp.where(jnp.arange(REQUESTS) == longest, MAXC, lengths).astype(jnp.int32)


def draw_page_table(key, part):
    first, second = jax.random.split(key, 2)
    devices = MAXP // KPG
    request_keys = jax.random.split(first, REQUESTS)
    orders = jax.vmap(lambda one: jax.random.permutation(one, devices))(request_keys)
    numbers = jnp.arange(MAXP)
    home = orders[:, numbers % devices]
    device_keys = jax.random.split(second, devices)
    shuffles = jax.vmap(lambda one: jax.random.permutation(one, SLOTS))(device_keys)
    local = jnp.arange(REQUESTS)[:, None] * KPG + numbers[None, :] // devices
    slot = shuffles[home, local]
    return (home * SLOTS + slot).astype(jnp.int32)


def levels(stream_key, shape, cuts, low, high):
    factor_of = 1.0
    for dim, parts in cuts:
        draws = jax.random.uniform(jax.random.fold_in(jax.random.fold_in(stream_key, 6), dim), (parts,), jnp.float32, low / len(cuts), high / len(cuts))
        factor_of = factor_of * jnp.repeat(jnp.exp(draws), shape[dim] // parts).reshape((-1,) + (1,) * (len(shape) - 1 - dim))
    return factor_of


def routed_block(rng, own, number, rows, count, top, bound, slope):
    ranking = jax.random.permutation(rng, count)
    crowded, ordinary = shares(count, rows * top, bound, slope, True), shares(count, rows * top, bound, slope, False)
    places = jnp.arange(count)

    def named(tallies, rotation):
        used = int((tallies > 0).sum())
        fixed = max(1, used // 4)
        passed = fixed + (places - fixed + rotation * (used - fixed)) % max(1, count - fixed)
        return jnp.zeros((count,), jnp.int32).at[ranking[jnp.where(places < fixed, places, passed)]].set(jnp.asarray(tallies, jnp.int32))

    tallies = jnp.where(number % 4 == 0, named(crowded, number // 4), named(ordinary, number - number // 4 - 1))
    mixed = jax.random.permutation(jax.random.fold_in(own, 3), count)
    donor, taker = mixed[0:count // 2 * 2:2], mixed[1:count // 2 * 2:2]
    room = jnp.minimum(tallies[donor] - 1, bound - tallies[taker]) // 2
    room = jnp.where((donor == ranking[0]) | (taker == ranking[0]) | (tallies[taker] == 0), 0, jnp.maximum(room, 0))
    passed = jax.random.randint(jax.random.fold_in(own, 4), (count // 2,), 0, 1 << 20) % (room + 1)
    tallies = tallies.at[donor].add(-passed).at[taker].add(passed)
    members = jnp.searchsorted(jnp.cumsum(tallies), jnp.arange(rows * top), side="right").astype(jnp.int32)
    table = members.reshape(top, rows).T
    table = table[jax.random.permutation(jax.random.fold_in(own, 1), rows)]
    rotation = jax.random.randint(jax.random.fold_in(own, 2), (rows, 1), 0, top)
    return jnp.take_along_axis(table, (jnp.arange(top)[None, :] + rotation) % top, axis=1)


def shares(count, total, reach, skew, full):
    portions = [(1 << 20) // math.isqrt(grade ** skew) + 1 for grade in range(1, count + 1)]
    largest = reach if full else min(reach, max(-(-total // count), total * portions[0] // sum(portions)))
    least = 1 if total - largest >= count - 1 else 0
    counts, surplus = [largest] + [least] * (count - 1), total - largest - least * (count - 1)
    while surplus > 0:
        free = [i for i in range(1, count) if counts[i] < largest] or [i for i in range(1, count) if counts[i] < reach]
        mass, budget = sum([portions[i] for i in free]), surplus
        for i in free:
            addition = min(reach - counts[i], max(1, budget * portions[i] // mass), surplus)
            counts[i] = counts[i] + addition
            surplus = surplus - addition
    return np.array(counts)


def bell_draw(rng, dims, scale, bound, cuts=(), kind=jnp.bfloat16):
    entries = jax.random.normal(rng, dims, jnp.float32) * scale
    if len(cuts) > 0:
        entries = levels(rng, dims, cuts, -0.22, 0.18) * entries
    return jnp.clip(entries, min=-bound, max=bound).astype(kind)


def setup_inputs(seed: int = 0) -> dict:
    seeds = jax.random.split(jax.random.key(seed), 15)
    x_resid = bell_draw(seeds[0], (TOKENS, D), 1.0, 6.0, ((0, 16), (1, 2)))
    q_new = draw_q_new(jax.random.fold_in(seeds[14], 71), 0)
    kv_new = bell_draw(seeds[2], (TOKENS, KVH, 2 * HEAD), 1.0, 4.0, ((0, 16), (1, 2)))
    kv_cache = draw_kv_cache(jax.random.fold_in(seeds[14], 71), 0)
    cache_len = draw_cache_len(jax.random.fold_in(seeds[14], 71), 0)
    page_table = draw_page_table(jax.random.fold_in(seeds[14], 71), 0)
    sinks = jnp.clip(8.0 * jax.random.uniform(seeds[6], (QH,), jnp.float32) ** levels(seeds[6], (QH,), ((0, 2),), -0.2, 0.2), 0.0, 8.0)
    out_weight = bell_draw(seeds[7], (QH * HEAD, D), (QH * HEAD) ** -0.5, 0.09375, ((0, 2),))
    norm_gain = jnp.clip(1.0 + 0.18 * jax.random.normal(seeds[8], (D,), jnp.float32), 0.1, 1.9)
    routes_keys = jax.random.split(jax.random.fold_in(seeds[9], 1), TOKENS // TOK_DEV)
    routes_turns = jax.random.permutation(jax.random.fold_in(seeds[9], 3), TOKENS // TOK_DEV)
    routes = jax.vmap(lambda own, number: routed_block(jax.random.fold_in(seeds[9], 2), own, number, TOK_DEV, EXPERTS, TOPK, CAP, 2))(routes_keys, routes_turns).reshape((TOKENS, TOPK))
    route_wt = jnp.clip(0.05 + 0.45 * jax.random.uniform(seeds[10], (TOKENS, TOPK), jnp.float32) ** levels(seeds[10], (TOKENS, TOPK), ((0, 16),), -0.2, 0.2), 0.05, 0.5)
    w_gate = bell_draw(seeds[11], (EXPERTS, D, EF), D ** -0.5, 0.109375, ((0, 16), (2, 2)))
    w_up = bell_draw(seeds[12], (EXPERTS, D, EF), D ** -0.5, 0.109375, ((0, 16), (2, 2)))
    w_down = bell_draw(seeds[13], (EXPERTS, EF, D), EF ** -0.5, 0.109375, ((0, 16), (1, 2)))
    return {"x_resid": x_resid, "q_new": q_new, "kv_new": kv_new, "kv_cache": kv_cache, "cache_len": cache_len, "page_table": page_table, "sinks": sinks, "out_weight": out_weight, "norm_gain": norm_gain, "routes": routes, "route_wt": route_wt, "w_gate": w_gate, "w_up": w_up, "w_down": w_down}


rope_base = 150000.0
neg_big = -1e+30
norm_eps = 1e-05

def rotate(values, where):
    half = values.shape[-1] // 2
    freq = rope_base ** (-jnp.arange(half, dtype=jnp.float32) * 2.0 / values.shape[-1])
    angle = where.astype(jnp.float32)[:, None] * freq[None, :]
    cosine = jnp.cos(angle)[:, None, :]
    sine = jnp.sin(angle)[:, None, :]
    first = values[..., :half]
    second = values[..., half:]
    return jnp.concatenate([first * cosine - second * sine, first * sine + second * cosine], -1)

def reference(x_resid, q_new, kv_new, kv_cache, cache_len, page_table, sinks, out_weight, norm_gain, routes, route_wt, w_gate, w_up, w_down):

    def one_request(request):
        length = cache_len[request]
        where = length + jnp.arange(NEW, dtype=jnp.int32)
        q_rows = lax.dynamic_slice_in_dim(q_new, request * NEW, NEW, 0).reshape(NEW, QH, HEAD)
        queries = rotate(q_rows.astype(jnp.float32), where).astype(jnp.bfloat16)
        kv_rows = lax.dynamic_slice_in_dim(kv_new, request * NEW, NEW, 0)
        new_keys = rotate(kv_rows[..., :HEAD].astype(jnp.float32), where).astype(jnp.bfloat16)
        pages = kv_cache[page_table[request]].reshape(MAXC, KVH, 2 * HEAD)
        keys = jnp.concatenate([pages[..., :HEAD], new_keys], 0)
        values = jnp.concatenate([pages[..., HEAD:], kv_rows[..., HEAD:]], 0)
        token = jnp.arange(NEW, dtype=jnp.int32)[:, None]
        entry = jnp.arange(MAXC + NEW, dtype=jnp.int32)[None, :]
        allowed = jnp.where(entry < MAXC, entry < length, entry - MAXC <= token)

        def one_head(group_head):
            q_head = lax.dynamic_slice_in_dim(queries, group_head * QPK, QPK, 1).astype(jnp.float32)
            k_head = keys[:, group_head].astype(jnp.float32)
            v_head = values[:, group_head].astype(jnp.float32)
            scores = jnp.einsum('ngd,kd->gnk', q_head, k_head) * HEAD ** (-0.5)
            scores = jnp.where(allowed[None], scores, neg_big)
            sink = lax.dynamic_slice_in_dim(sinks, group_head * QPK, QPK)[:, None]
            top = jnp.maximum(lax.optimization_barrier(jnp.max(scores, -1)), sink)
            expo = jnp.exp(scores - top[..., None])
            weights = lax.optimization_barrier(expo.astype(jnp.bfloat16)).astype(jnp.float32)
            total = lax.optimization_barrier(jnp.sum(expo, -1)) + jnp.exp(sink - top)
            result = jnp.einsum('gnk,kd->gnd', weights, v_head) / total[..., None]
            return result.astype(jnp.bfloat16)
        heads = lax.map(one_head, jnp.arange(KVH, dtype=jnp.int32))
        return heads.transpose(2, 0, 1, 3).reshape(NEW, QH * HEAD)
    attended = lax.map(one_request, jnp.arange(REQUESTS, dtype=jnp.int32)).reshape(TOKENS, QH * HEAD)
    resid = (x_resid.astype(jnp.float32) + jnp.dot(attended, out_weight, preferred_element_type=jnp.float32)).astype(jnp.bfloat16)
    resid_wide = resid.astype(jnp.float32)
    scale_rows = lax.rsqrt(lax.optimization_barrier(jnp.mean(resid_wide * resid_wide, -1, keepdims=True)) + norm_eps)
    normed = (resid_wide * scale_rows * norm_gain[None, :]).astype(jnp.bfloat16)
    flat = routes.reshape(N_SEQ, TOK_DEV * TOPK)
    onehot = (flat[..., None] == jnp.arange(EXPERTS, dtype=jnp.int32)).astype(jnp.int32)
    running = (jnp.cumsum(onehot, 1) - 1).astype(jnp.int32)
    rank = lax.optimization_barrier(jnp.sum(onehot * running, -1)).astype(jnp.int32)
    block = jnp.broadcast_to(jnp.arange(N_SEQ, dtype=jnp.int32)[:, None], flat.shape)
    token_of = block * TOK_DEV + jnp.broadcast_to(jnp.arange(TOK_DEV * TOPK, dtype=jnp.int32)[None, :] // TOPK, flat.shape)
    source = jnp.full((EXPERTS, N_SEQ, CAP), TOKENS, jnp.int32).at[flat, block, rank].set(token_of.astype(jnp.int32))
    padded = jnp.concatenate([normed, jnp.zeros((1, D), jnp.bfloat16)], 0)

    def one_expert(expert):
        rows_in = padded[source[expert].reshape(-1)]
        hidden = jnp.dot(rows_in, w_gate[expert], preferred_element_type=jnp.float32)
        lin = jnp.dot(rows_in, w_up[expert], preferred_element_type=jnp.float32)
        act = (hidden * jax.nn.sigmoid(1.702 * hidden) * (lin + 1.0)).astype(jnp.bfloat16)
        pieces = jnp.einsum('rjf,jfd->jrd', act.reshape(N_SEQ * CAP, N_TP, EF // N_TP).astype(jnp.float32), w_down[expert].reshape(N_TP, EF // N_TP, D).astype(jnp.float32))
        pieces = lax.optimization_barrier(pieces.astype(jnp.bfloat16)).astype(jnp.float32)
        return lax.optimization_barrier(jnp.sum(pieces, 0)).astype(jnp.bfloat16)
    expert_out = lax.map(one_expert, jnp.arange(EXPERTS, dtype=jnp.int32)).reshape(EXPERTS * N_SEQ * CAP, D)
    position = (flat * (N_SEQ * CAP) + block * CAP + rank).reshape(TOKENS, TOPK).astype(jnp.int32)
    taken = expert_out[position].astype(jnp.float32)
    mixture = lax.optimization_barrier(jnp.sum(route_wt[..., None] * taken, 1))
    output = (resid_wide + mixture).astype(jnp.bfloat16)
    return (attended, output)
```

```python
import jax
import jax.numpy as jnp
from jax import lax
from jax.sharding import PartitionSpec as P

D = 2880
NEW = 128


rope_base = 150000.0
neg_big = -1e30
norm_eps = 1e-05


def rotate(values, where):
    half = values.shape[-1] // 2
    freq = rope_base ** (-jnp.arange(half, dtype=jnp.float32) * 2.0 / values.shape[-1])
    angle = where.astype(jnp.float32)[:, None] * freq[None, :]
    cosine = jnp.cos(angle)[:, None, :]
    sine = jnp.sin(angle)[:, None, :]
    first = values[..., :half]
    second = values[..., half:]
    return jnp.concatenate([first * cosine - second * sine, first * sine + second * cosine], -1)


def per_device(
    x_resid,
    q_new,
    kv_new,
    kv_cache,
    cache_len,
    page_table,
    sinks,
    out_weight,
    norm_gain,
    routes,
    route_wt,
    w_gate,
    w_up,
    w_down,
):
    seq_count = lax.axis_size("seq")
    seq_here = lax.axis_index("seq")
    tp_here = lax.axis_index("tp")
    rows, cols = x_resid.shape
    local_kv = kv_new.shape[1]
    head = kv_new.shape[2] // 2
    local_q = q_new.shape[1] // head
    group = local_q // local_kv
    slots = kv_cache.shape[0]
    page = kv_cache.shape[1]
    requests, max_pages = page_table.shape
    topk = routes.shape[1]
    request_ids = jnp.arange(requests, dtype=jnp.int32)
    is_own = (request_ids == seq_here).astype(jnp.int32)
    length = jnp.sum(is_own * cache_len)
    kpg = slots // requests
    home = page_table // slots
    spot = page_table % slots
    here = (home == seq_here).astype(jnp.int32)
    earlier = jnp.cumsum(here, 1) - here
    order = jnp.sum(
        (here * spot)[:, None, :]
        * (earlier[:, None, :] == jnp.arange(kpg, dtype=jnp.int32)[None, :, None]),
        2,
    )
    leaving = kv_cache[order.reshape(-1)].reshape(seq_count, kpg * page, local_kv * 2 * head)
    pages = lax.all_to_all(leaving, "seq", split_axis=0, concat_axis=0, tiled=True)
    pages = pages.reshape(seq_count * kpg * page, local_kv, 2 * head).transpose(1, 0, 2)
    own_home = jnp.sum(is_own[:, None] * home, 0)
    numbers = jnp.arange(max_pages, dtype=jnp.int32)
    before = (own_home[None, :] == own_home[:, None]) & (numbers[None, :] < numbers[:, None])
    arrival = own_home * kpg + jnp.sum(before.astype(jnp.int32), 1)
    page_num = jnp.sum((arrival[None, :] == numbers[:, None]) * numbers[None, :], 1)
    entry = (page_num[:, None] * page + jnp.arange(page, dtype=jnp.int32)[None, :]).reshape(-1)

    row_off = jnp.arange(rows, dtype=jnp.int32)
    where = length + row_off
    rotated = rotate(q_new.reshape(rows, local_q, head).astype(jnp.float32), where).astype(
        jnp.bfloat16
    )
    queries = (
        rotated.reshape(rows, local_kv, group, head)
        .transpose(1, 0, 2, 3)
        .reshape(local_kv, rows * group, head)
    )
    fresh_keys = rotate(kv_new[..., :head].astype(jnp.float32), where).astype(jnp.bfloat16)
    fresh = jnp.concatenate([fresh_keys, kv_new[..., head:]], -1).transpose(1, 0, 2)
    sink_rows = jnp.broadcast_to(
        sinks.reshape(local_kv, 1, group), (local_kv, rows, group)
    ).reshape(local_kv, rows * group)
    both = jnp.concatenate([pages, fresh], 1)
    past = jnp.broadcast_to((entry < length)[None, :], (rows, entry.shape[0]))
    allowed = jnp.concatenate([past, row_off[None, :] <= row_off[:, None]], 1)
    bias = jnp.where(jnp.repeat(allowed, group, axis=0), 0.0, neg_big)
    scores = jnp.einsum(
        "hqd,hkd->hqk", queries, both[..., :head], preferred_element_type=jnp.float32
    ) * head ** (-0.5)
    scores = jnp.where(bias[None] < 0.0, neg_big, scores)
    top = jnp.maximum(jnp.max(scores, -1), sink_rows)
    expo = jnp.exp(scores - top[..., None])
    total = jnp.sum(expo, -1) + jnp.exp(sink_rows - top)
    summed = jnp.einsum(
        "hqk,hkd->hqd",
        expo.astype(jnp.bfloat16),
        both[..., head:],
        preferred_element_type=jnp.float32,
    )
    attended = (summed / total[..., None]).astype(jnp.bfloat16)
    attended = (
        attended.reshape(local_kv, rows, group, head)
        .transpose(1, 0, 2, 3)
        .reshape(rows, local_q * head)
    )
    output = after_attention(
        attended, x_resid, out_weight, norm_gain, routes, route_wt, w_gate, w_up, w_down
    )
    return (attended, output)


def after_attention(
    attended, x_resid, out_weight, norm_gain, routes, route_wt, w_gate, w_up, w_down
):
    seq_count = lax.axis_size("seq")
    tp_count = lax.axis_size("tp")
    tp_here = lax.axis_index("tp")
    rows, cols = x_resid.shape
    topk = routes.shape[1]
    experts_all = w_gate.shape[0] * seq_count
    cap = 2 * rows * topk // experts_all
    flat_routes = routes.reshape(-1)
    onehot = (flat_routes[:, None] == jnp.arange(experts_all, dtype=jnp.int32)[None, :]).astype(
        jnp.int32
    )
    rank = jnp.sum(onehot * (jnp.cumsum(onehot, 0) - 1), 1)
    slot = (flat_routes * cap + rank).reshape(rows, topk)
    slot_ids = jnp.arange(experts_all * cap, dtype=jnp.int32)[:, None]
    place = jnp.zeros((experts_all * cap, rows), jnp.float32)
    weigh = jnp.zeros((experts_all * cap, rows), jnp.float32)
    for j in range(topk):
        same = slot_ids == slot[:, j][None, :]
        place = jnp.where(same, 1.0, place)
        weigh = jnp.where(same, route_wt[:, j][None, :], weigh)
    place = place.astype(jnp.bfloat16)
    weigh_high = lax.reduce_precision(weigh, 8, 7)
    weigh_low = (weigh - weigh_high).astype(jnp.bfloat16)
    weigh_high = weigh_high.astype(jnp.bfloat16)

    partial_value = jnp.dot(attended, out_weight, preferred_element_type=jnp.float32)
    gain_here = lax.dynamic_slice_in_dim(norm_gain, tp_here * cols, cols)
    column_sums = lax.psum_scatter(
        partial_value.astype(jnp.bfloat16), "tp", scatter_dimension=1, tiled=True
    ).astype(jnp.float32)
    resid = (x_resid.astype(jnp.float32) + column_sums).astype(jnp.bfloat16)
    resid_wide = resid.astype(jnp.float32)
    squares = lax.psum(jnp.sum(resid_wide * resid_wide, 1), "tp")
    scale_rows = lax.rsqrt(squares / D + norm_eps)
    normed_cols = (resid_wide * scale_rows[:, None] * gain_here[None, :]).astype(jnp.bfloat16)
    outgoing = jnp.dot(place, normed_cols, preferred_element_type=jnp.float32).astype(jnp.bfloat16)
    arrived_cols = lax.all_to_all(
        outgoing.reshape(seq_count, cap, cols), "seq", split_axis=0, concat_axis=0, tiled=True
    ).reshape(seq_count * cap, cols)
    arrived = lax.all_gather(arrived_cols, "tp", axis=0, tiled=False)
    hidden = 0.0
    lin = 0.0
    for t in range(tp_count):
        part = slice(t * cols, (t + 1) * cols)
        hidden = hidden + jnp.dot(arrived[t], w_gate[0, part], preferred_element_type=jnp.float32)
        lin = lin + jnp.dot(arrived[t], w_up[0, part], preferred_element_type=jnp.float32)
    act = (hidden * jax.nn.sigmoid(1.702 * hidden) * (lin + 1.0)).astype(jnp.bfloat16)
    if tp_count == 2:
        start = cols // 128 * 128
        width = D - start
        low = jnp.dot(act, w_down[0, :, :width], preferred_element_type=jnp.float32)
        high = jnp.dot(act, w_down[0, :, start:], preferred_element_type=jnp.float32)
        low = low.astype(jnp.bfloat16)
        high = high.astype(jnp.bfloat16)
        first = tp_here == 0
        taken = lax.ppermute(jnp.where(first, high, low), "tp", [(0, 1), (1, 0)])
        kept = jnp.where(first, low, high)
        expert_out = (kept.astype(jnp.float32) + taken.astype(jnp.float32)).astype(jnp.bfloat16)
    else:
        down = jnp.dot(act, w_down[0], preferred_element_type=jnp.float32)
        expert_out = lax.psum_scatter(
            down.astype(jnp.bfloat16), "tp", scatter_dimension=1, tiled=True
        )
        width = cols
    returned = lax.all_to_all(
        expert_out.reshape(seq_count, cap, width), "seq", split_axis=0, concat_axis=0, tiled=True
    ).reshape(experts_all * cap, width)
    mixture = sum(
        lax.dot_general(
            part, returned, (((0,), (0,)), ((), ())), preferred_element_type=jnp.float32
        )
        for part in (weigh_high, weigh_low)
    )
    if tp_count == 2:
        mixture = jnp.where(first, mixture[:, :cols], mixture[:, cols - start : 2 * cols - start])
    return (resid_wide + mixture).astype(jnp.bfloat16)


def solution(mesh):
    in_specs = (
        P("seq", "tp"),
        P("seq", "tp"),
        P("seq", "tp", None),
        P("seq", None, "tp", None),
        P(),
        P(),
        P("tp"),
        P("tp", None),
        P(),
        P("seq", None),
        P("seq", None),
        P("seq", None, "tp"),
        P("seq", None, "tp"),
        P("seq", "tp", None),
    )
    out_specs = (P("seq", "tp"), P("seq", "tp"))
    return jax.shard_map(
        per_device, mesh=mesh, in_specs=in_specs, out_specs=out_specs, check_vma=False
    )
```

```python
import jax
import jax.numpy as jnp
from jax import lax
from jax.sharding import PartitionSpec as P

D = 2880
NEW = 128


rope_base = 150000.0
neg_big = -1e30
norm_eps = 1e-05
chunk_count = 2


def rotate(values, where):
    half = values.shape[-1] // 2
    freq = rope_base ** (-jnp.arange(half, dtype=jnp.float32) * 2.0 / values.shape[-1])
    angle = where.astype(jnp.float32)[:, None] * freq[None, :]
    cosine = jnp.cos(angle)[:, None, :]
    sine = jnp.sin(angle)[:, None, :]
    first = values[..., :half]
    second = values[..., half:]
    return jnp.concatenate([first * cosine - second * sine, first * sine + second * cosine], -1)


def per_device(
    x_resid,
    q_new,
    kv_new,
    kv_cache,
    cache_len,
    page_table,
    sinks,
    out_weight,
    norm_gain,
    routes,
    route_wt,
    w_gate,
    w_up,
    w_down,
):
    seq_count = lax.axis_size("seq")
    seq_here = lax.axis_index("seq")
    tp_here = lax.axis_index("tp")
    rows, cols = x_resid.shape
    local_kv = kv_new.shape[1]
    head = kv_new.shape[2] // 2
    local_q = q_new.shape[1] // head
    group = local_q // local_kv
    slots = kv_cache.shape[0]
    page = kv_cache.shape[1]
    requests, max_pages = page_table.shape
    topk = routes.shape[1]
    request_ids = jnp.arange(requests, dtype=jnp.int32)
    is_own = (request_ids == seq_here).astype(jnp.int32)
    length = jnp.sum(is_own * cache_len)
    kpg = slots // requests
    home = page_table // slots
    spot = page_table % slots
    here = (home == seq_here).astype(jnp.int32)
    earlier = jnp.cumsum(here, 1) - here
    order = jnp.sum(
        (here * spot)[:, None, :]
        * (earlier[:, None, :] == jnp.arange(kpg, dtype=jnp.int32)[None, :, None]),
        2,
    )
    leaving = kv_cache[order.reshape(-1)].reshape(seq_count, kpg * page, local_kv * 2 * head)
    pages = lax.all_to_all(leaving, "seq", split_axis=0, concat_axis=0, tiled=True)
    pages = pages.reshape(seq_count * kpg * page, local_kv, 2 * head).transpose(1, 0, 2)
    own_home = jnp.sum(is_own[:, None] * home, 0)
    numbers = jnp.arange(max_pages, dtype=jnp.int32)
    before = (own_home[None, :] == own_home[:, None]) & (numbers[None, :] < numbers[:, None])
    arrival = own_home * kpg + jnp.sum(before.astype(jnp.int32), 1)
    page_num = jnp.sum((arrival[None, :] == numbers[:, None]) * numbers[None, :], 1)
    entry = (page_num[:, None] * page + jnp.arange(page, dtype=jnp.int32)[None, :]).reshape(-1)

    row_off = jnp.arange(rows, dtype=jnp.int32)
    where = length + row_off
    rotated = rotate(q_new.reshape(rows, local_q, head).astype(jnp.float32), where).astype(
        jnp.bfloat16
    )
    queries = (
        rotated.reshape(rows, local_kv, group, head)
        .transpose(1, 0, 2, 3)
        .reshape(local_kv, rows * group, head)
    )
    fresh_keys = rotate(kv_new[..., :head].astype(jnp.float32), where).astype(jnp.bfloat16)
    fresh = jnp.concatenate([fresh_keys, kv_new[..., head:]], -1).transpose(1, 0, 2)
    sink_rows = jnp.broadcast_to(
        sinks.reshape(local_kv, 1, group), (local_kv, rows, group)
    ).reshape(local_kv, rows * group)
    both = jnp.concatenate([pages, fresh], 1)
    past = jnp.broadcast_to((entry < length)[None, :], (rows, entry.shape[0]))
    allowed = jnp.concatenate([past, row_off[None, :] <= row_off[:, None]], 1)
    bias = jnp.where(jnp.repeat(allowed, group, axis=0), 0.0, neg_big)
    scores = jnp.einsum(
        "hqd,hkd->hqk", queries, both[..., :head], preferred_element_type=jnp.float32
    ) * head ** (-0.5)
    scores = jnp.where(bias[None] < 0.0, neg_big, scores)
    top = jnp.maximum(jnp.max(scores, -1), sink_rows)
    expo = jnp.exp(scores - top[..., None])
    total = jnp.sum(expo, -1) + jnp.exp(sink_rows - top)
    summed = jnp.einsum(
        "hqk,hkd->hqd",
        expo.astype(jnp.bfloat16),
        both[..., head:],
        preferred_element_type=jnp.float32,
    )
    attended = (summed / total[..., None]).astype(jnp.bfloat16)
    attended = (
        attended.reshape(local_kv, rows, group, head)
        .transpose(1, 0, 2, 3)
        .reshape(rows, local_q * head)
    )
    output = after_attention(
        attended, x_resid, out_weight, norm_gain, routes, route_wt, w_gate, w_up, w_down
    )
    return (attended, output)


def after_attention(
    attended, x_resid, out_weight, norm_gain, routes, route_wt, w_gate, w_up, w_down
):
    seq_count = lax.axis_size("seq")
    tp_count = lax.axis_size("tp")
    tp_here = lax.axis_index("tp")
    rows, cols = x_resid.shape
    topk = routes.shape[1]
    experts_all = w_gate.shape[0] * seq_count
    cap = 2 * rows * topk // experts_all
    part = cap // (chunk_count * tp_count)
    flat_routes = routes.reshape(-1)
    onehot = (flat_routes[:, None] == jnp.arange(experts_all, dtype=jnp.int32)[None, :]).astype(
        jnp.int32
    )
    rank = jnp.sum(onehot * (jnp.cumsum(onehot, 0) - 1), 1)
    expert_ids = jnp.arange(experts_all, dtype=jnp.int32)[:, None]
    part_ids = jnp.arange(part, dtype=jnp.int32)[None, :]
    slot = (flat_routes * cap + rank).reshape(rows, topk)
    places = []
    weighs = []
    for c in range(chunk_count):
        ids = expert_ids * cap + (c * tp_count + tp_here) * part + part_ids
        ids = ids.reshape(-1, 1)
        place = jnp.zeros((experts_all * part, rows), jnp.float32)
        weigh = jnp.zeros((experts_all * part, rows), jnp.float32)
        for j in range(topk):
            same = ids == slot[:, j][None, :]
            place = jnp.where(same, 1.0, place)
            weigh = jnp.where(same, route_wt[:, j][None, :], weigh)
        high = lax.reduce_precision(weigh, 8, 7)
        low = (weigh - high).astype(jnp.bfloat16)
        places.append(place.astype(jnp.bfloat16))
        weighs.append((high.astype(jnp.bfloat16), low))

    partial_value = jnp.dot(attended, out_weight, preferred_element_type=jnp.float32)
    gain_here = lax.dynamic_slice_in_dim(norm_gain, tp_here * cols, cols)
    column_sums = lax.psum_scatter(
        partial_value.astype(jnp.bfloat16), "tp", scatter_dimension=1, tiled=True
    ).astype(jnp.float32)
    resid = (x_resid.astype(jnp.float32) + column_sums).astype(jnp.bfloat16)
    resid_wide = resid.astype(jnp.float32)
    squares = lax.psum(jnp.sum(resid_wide * resid_wide, 1), "tp")
    scale_rows = lax.rsqrt(squares / D + norm_eps)
    normed_cols = (resid_wide * scale_rows[:, None] * gain_here[None, :]).astype(jnp.bfloat16)
    normed = lax.all_gather(normed_cols, "tp", axis=1, tiled=True)

    def exchange(block):
        return lax.all_to_all(
            block.reshape(seq_count, part, D), "seq", split_axis=0, concat_axis=0, tiled=True
        ).reshape(seq_count * part, D)

    swap = [(0, 1), (1, 0)]
    arrived = []
    for c in range(chunk_count):
        leaving = jnp.dot(places[c], normed, preferred_element_type=jnp.float32)
        arrived.append(exchange(leaving.astype(jnp.bfloat16)))
    mixture = 0.0
    for c in range(chunk_count):
        own = arrived[c]
        if tp_count == 2:
            block = jnp.concatenate([own, lax.ppermute(own, "tp", swap)], 0)
        else:
            block = lax.all_gather(own, "tp", axis=0, tiled=True)
        hidden = jnp.dot(block, w_gate[0], preferred_element_type=jnp.float32)
        lin = jnp.dot(block, w_up[0], preferred_element_type=jnp.float32)
        act = (hidden * jax.nn.sigmoid(1.702 * hidden) * (lin + 1.0)).astype(jnp.bfloat16)
        if tp_count == 2:
            count = own.shape[0]
            other = jnp.dot(act[count:], w_down[0], preferred_element_type=jnp.float32)
            other = lax.ppermute(other.astype(jnp.bfloat16), "tp", swap)
            mine = jnp.dot(act[:count], w_down[0], preferred_element_type=jnp.float32)
            mine = mine.astype(jnp.bfloat16)
            total = mine.astype(jnp.float32) + other.astype(jnp.float32)
            expert_out = total.astype(jnp.bfloat16)
        else:
            down = jnp.dot(act, w_down[0], preferred_element_type=jnp.float32)
            expert_out = lax.psum_scatter(
                down.astype(jnp.bfloat16), "tp", scatter_dimension=0, tiled=True
            )
        returned = exchange(expert_out)
        for share in weighs[c]:
            mixture = mixture + lax.dot_general(
                share, returned, (((0,), (0,)), ((), ())), preferred_element_type=jnp.float32
            )
    mixture = lax.psum_scatter(mixture, "tp", scatter_dimension=1, tiled=True)
    return (resid_wide + mixture).astype(jnp.bfloat16)


def solution(mesh):
    in_specs = (
        P("seq", "tp"),
        P("seq", "tp"),
        P("seq", "tp", None),
        P("seq", None, "tp", None),
        P(),
        P(),
        P("tp"),
        P("tp", None),
        P(),
        P("seq", None),
        P("seq", None),
        P("seq", None, "tp"),
        P("seq", None, "tp"),
        P("seq", "tp", None),
    )
    out_specs = (P("seq", "tp"), P("seq", "tp"))
    return jax.shard_map(
        per_device, mesh=mesh, in_specs=in_specs, out_specs=out_specs, check_vma=False
    )
```

```python
import jax
import jax.numpy as jnp
from jax import lax
from jax.sharding import PartitionSpec as P

D = 2880
NEW = 128


rope_base = 150000.0
neg_big = -1e30
norm_eps = 1e-05
chunk_count = 2


def rotate(values, where):
    half = values.shape[-1] // 2
    freq = rope_base ** (-jnp.arange(half, dtype=jnp.float32) * 2.0 / values.shape[-1])
    angle = where.astype(jnp.float32)[:, None] * freq[None, :]
    cosine = jnp.cos(angle)[:, None, :]
    sine = jnp.sin(angle)[:, None, :]
    first = values[..., :half]
    second = values[..., half:]
    return jnp.concatenate([first * cosine - second * sine, first * sine + second * cosine], -1)


def per_device(
    x_resid,
    q_new,
    kv_new,
    kv_cache,
    cache_len,
    page_table,
    sinks,
    out_weight,
    norm_gain,
    routes,
    route_wt,
    w_gate,
    w_up,
    w_down,
):
    seq_count = lax.axis_size("seq")
    seq_here = lax.axis_index("seq")
    tp_here = lax.axis_index("tp")
    rows, cols = x_resid.shape
    local_kv = kv_new.shape[1]
    head = kv_new.shape[2] // 2
    local_q = q_new.shape[1] // head
    group = local_q // local_kv
    slots = kv_cache.shape[0]
    page = kv_cache.shape[1]
    requests, max_pages = page_table.shape
    topk = routes.shape[1]
    request_ids = jnp.arange(requests, dtype=jnp.int32)
    is_own = (request_ids == seq_here).astype(jnp.int32)
    length = jnp.sum(is_own * cache_len)
    kpg = slots // requests
    home = page_table // slots
    spot = page_table % slots
    here = (home == seq_here).astype(jnp.int32)
    earlier = jnp.cumsum(here, 1) - here
    order = jnp.sum(
        (here * spot)[:, None, :]
        * (earlier[:, None, :] == jnp.arange(kpg, dtype=jnp.int32)[None, :, None]),
        2,
    )
    leaving = kv_cache[order.reshape(-1)].reshape(seq_count, kpg * page, local_kv * 2 * head)
    pages = lax.all_to_all(leaving, "seq", split_axis=0, concat_axis=0, tiled=True)
    pages = pages.reshape(seq_count * kpg * page, local_kv, 2 * head).transpose(1, 0, 2)
    own_home = jnp.sum(is_own[:, None] * home, 0)
    numbers = jnp.arange(max_pages, dtype=jnp.int32)
    before = (own_home[None, :] == own_home[:, None]) & (numbers[None, :] < numbers[:, None])
    arrival = own_home * kpg + jnp.sum(before.astype(jnp.int32), 1)
    page_num = jnp.sum((arrival[None, :] == numbers[:, None]) * numbers[None, :], 1)
    entry = (page_num[:, None] * page + jnp.arange(page, dtype=jnp.int32)[None, :]).reshape(-1)

    row_off = jnp.arange(rows, dtype=jnp.int32)
    where = length + row_off
    rotated = rotate(q_new.reshape(rows, local_q, head).astype(jnp.float32), where).astype(
        jnp.bfloat16
    )
    queries = (
        rotated.reshape(rows, local_kv, group, head)
        .transpose(1, 0, 2, 3)
        .reshape(local_kv, rows * group, head)
    )
    fresh_keys = rotate(kv_new[..., :head].astype(jnp.float32), where).astype(jnp.bfloat16)
    fresh = jnp.concatenate([fresh_keys, kv_new[..., head:]], -1).transpose(1, 0, 2)
    sink_rows = jnp.broadcast_to(
        sinks.reshape(local_kv, 1, group), (local_kv, rows, group)
    ).reshape(local_kv, rows * group)
    both = jnp.concatenate([pages, fresh], 1)
    past = jnp.broadcast_to((entry < length)[None, :], (rows, entry.shape[0]))
    allowed = jnp.concatenate([past, row_off[None, :] <= row_off[:, None]], 1)
    bias = jnp.where(jnp.repeat(allowed, group, axis=0), 0.0, neg_big)
    parts = []
    for g in range(local_kv):
        scores = jnp.dot(
            queries[g], both[g, :, :head].T, preferred_element_type=jnp.float32
        ) * head ** (-0.5)
        scores = jnp.where(bias < 0.0, neg_big, scores)
        top = jnp.maximum(jnp.max(scores, -1), sink_rows[g])
        expo = jnp.exp(scores - top[:, None])
        total = jnp.sum(expo, -1) + jnp.exp(sink_rows[g] - top)
        summed = jnp.dot(
            expo.astype(jnp.bfloat16), both[g, :, head:], preferred_element_type=jnp.float32
        )
        parts.append((summed / total[:, None]).astype(jnp.bfloat16))
    attended = jnp.stack(parts)
    attended = (
        attended.reshape(local_kv, rows, group, head)
        .transpose(1, 0, 2, 3)
        .reshape(rows, local_q * head)
    )
    output = after_attention(
        attended, x_resid, out_weight, norm_gain, routes, route_wt, w_gate, w_up, w_down
    )
    return (attended, output)


def after_attention(
    attended, x_resid, out_weight, norm_gain, routes, route_wt, w_gate, w_up, w_down
):
    seq_count = lax.axis_size("seq")
    tp_count = lax.axis_size("tp")
    tp_here = lax.axis_index("tp")
    rows, cols = x_resid.shape
    topk = routes.shape[1]
    experts_all = w_gate.shape[0] * seq_count
    cap = 2 * rows * topk // experts_all
    part = cap // (chunk_count * tp_count)
    flat_routes = routes.reshape(-1)
    onehot = (flat_routes[:, None] == jnp.arange(experts_all, dtype=jnp.int32)[None, :]).astype(
        jnp.int32
    )
    rank = jnp.sum(onehot * (jnp.cumsum(onehot, 0) - 1), 1)
    expert_ids = jnp.arange(experts_all, dtype=jnp.int32)[:, None]
    part_ids = jnp.arange(part, dtype=jnp.int32)[None, :]
    slot = (flat_routes * cap + rank).reshape(rows, topk)
    places = []
    weighs = []
    for c in range(chunk_count):
        ids = expert_ids * cap + (c * tp_count + tp_here) * part + part_ids
        ids = ids.reshape(-1, 1)
        place = jnp.zeros((experts_all * part, rows), jnp.float32)
        weigh = jnp.zeros((experts_all * part, rows), jnp.float32)
        for j in range(topk):
            same = ids == slot[:, j][None, :]
            place = jnp.where(same, 1.0, place)
            weigh = jnp.where(same, route_wt[:, j][None, :], weigh)
        high = lax.reduce_precision(weigh, 8, 7)
        low = (weigh - high).astype(jnp.bfloat16)
        places.append(place.astype(jnp.bfloat16))
        weighs.append((high.astype(jnp.bfloat16), low))

    partial_value = jnp.dot(attended, out_weight, preferred_element_type=jnp.float32)
    gain_here = lax.dynamic_slice_in_dim(norm_gain, tp_here * cols, cols)
    column_sums = lax.psum_scatter(
        partial_value.astype(jnp.bfloat16), "tp", scatter_dimension=1, tiled=True
    ).astype(jnp.float32)
    resid = (x_resid.astype(jnp.float32) + column_sums).astype(jnp.bfloat16)
    resid_wide = resid.astype(jnp.float32)
    squares = lax.psum(jnp.sum(resid_wide * resid_wide, 1), "tp")
    scale_rows = lax.rsqrt(squares / D + norm_eps)
    normed_cols = (resid_wide * scale_rows[:, None] * gain_here[None, :]).astype(jnp.bfloat16)
    normed = lax.all_gather(normed_cols, "tp", axis=1, tiled=True)

    def exchange(block):
        return lax.all_to_all(
            block.reshape(seq_count, part, D), "seq", split_axis=0, concat_axis=0, tiled=True
        ).reshape(seq_count * part, D)

    swap = [(0, 1), (1, 0)]
    arrived = []
    for c in range(chunk_count):
        leaving = jnp.dot(places[c], normed, preferred_element_type=jnp.float32)
        arrived.append(exchange(leaving.astype(jnp.bfloat16)))
    returned = []
    expert_out = None
    for c in range(chunk_count):
        own = arrived[c]
        if tp_count == 2:
            pair = lax.ppermute(own, "tp", swap)
            if expert_out is not None:
                own, pair, expert_out = lax.optimization_barrier((own, pair, expert_out))
                returned.append(exchange(expert_out))
            block = jnp.concatenate([own, pair], 0)
        else:
            block = lax.all_gather(own, "tp", axis=0, tiled=True)
            if expert_out is not None:
                block, expert_out = lax.optimization_barrier((block, expert_out))
                returned.append(exchange(expert_out))
        hidden = jnp.dot(block, w_gate[0], preferred_element_type=jnp.float32)
        lin = jnp.dot(block, w_up[0], preferred_element_type=jnp.float32)
        act = (hidden * jax.nn.sigmoid(1.702 * hidden) * (lin + 1.0)).astype(jnp.bfloat16)
        if tp_count == 2:
            count = own.shape[0]
            other = jnp.dot(act[count:], w_down[0], preferred_element_type=jnp.float32)
            other = lax.ppermute(other.astype(jnp.bfloat16), "tp", swap)
            mine = jnp.dot(act[:count], w_down[0], preferred_element_type=jnp.float32)
            mine = mine.astype(jnp.bfloat16)
            total = mine.astype(jnp.float32) + other.astype(jnp.float32)
            expert_out = total.astype(jnp.bfloat16)
        else:
            down = jnp.dot(act, w_down[0], preferred_element_type=jnp.float32)
            expert_out = lax.psum_scatter(
                down.astype(jnp.bfloat16), "tp", scatter_dimension=0, tiled=True
            )
    returned.append(exchange(expert_out))
    mixture = 0.0
    for shares, rows_back in zip(weighs, returned):
        for share in shares:
            mixture = mixture + lax.dot_general(
                share, rows_back, (((0,), (0,)), ((), ())), preferred_element_type=jnp.float32
            )
    mixture = lax.psum_scatter(mixture, "tp", scatter_dimension=1, tiled=True)
    return (resid_wide + mixture).astype(jnp.bfloat16)


def solution(mesh):
    in_specs = (
        P("seq", "tp"),
        P("seq", "tp"),
        P("seq", "tp", None),
        P("seq", None, "tp", None),
        P(),
        P(),
        P("tp"),
        P("tp", None),
        P(),
        P("seq", None),
        P("seq", None),
        P("seq", None, "tp"),
        P("seq", None, "tp"),
        P("seq", "tp", None),
    )
    out_specs = (P("seq", "tp"), P("seq", "tp"))
    return jax.shard_map(
        per_device, mesh=mesh, in_specs=in_specs, out_specs=out_specs, check_vma=False
    )
```
